128 devices in a mesh: dp: 16 (over z_hi, x, core), tensor: 8 (over y, z_lo).
Axes of the slice: x: 4, y: 4, z: 4 (z_hi: 2, z_lo: 2; z = z_hi * 2 + z_lo), core: 2. Of those that a mesh axis runs over, the one named last changes fastest.
Arguments:
- partial_grads: bfloat16 [16, 1024, 28672], P('dp', None, 'tensor'), may hold values from -6 to 6
- master: float32 [1024, 28672], P(('dp', 'tensor')), may hold values from -6 to 6
- first_moment: float32 [1024, 28672], P(('dp', 'tensor')), may hold values from -6 to 6
- second_moment: float32 [1024, 28672], P(('dp', 'tensor')), may hold values from 0.01 to 4
- noise_draws: bfloat16 [16, 1024, 28672], P(None, ('dp', 'tensor')), may hold values from -6 to 6
- band_coeffs: int32 [16], replicated, may hold values from 1 to 32
- step: int32 [1], replicated, may hold values from 0 to 15
Outputs:
- new_master: float32 [1024, 28672], P(('dp', 'tensor'))
- new_first: float32 [1024, 28672], P(('dp', 'tensor'))
- new_second: float32 [1024, 28672], P(('dp', 'tensor'))
- weights: bfloat16 [1024, 28672], P(None, 'tensor')
The draws below stay inside these ranges and needn't reach their ends.
All inputs are finite; a program needn't handle non-finite values.
Results may differ from the reference program's by a relative error of at most 0.0035.
Values may be sent and summed in bfloat16 or wider, within the bound.
No kernel may reach another device: no remote copies, remote signals or barrier semaphores. Data moves between devices by JAX's collectives and lax.ppermute only.
A program may use at most 128 MiB of HBM per device.

```python
import math
import jax
import jax.numpy as jnp
from jax import lax

FF = 28672
HISTORY = 16
ROWS = 1024
N_DP = 16


def touch_ends(values, key, least, top_value):
    extent = values.shape
    spot = [jax.random.randint(jax.random.fold_in(key, axis), (), 0, extent[axis]) for axis in range(len(extent))]
    values = values.at[tuple(spot)].set(least)
    longest = extent.index(max(extent))
    spot[longest] = (spot[longest] + 1) % extent[longest]
    return values.at[tuple(spot)].set(top_value)


def spiked(entries, key, source, target, blocks, factor):
    def block_of(position):
        return (jnp.arange(entries.shape[position]) // (entries.shape[position] // blocks)).reshape((-1,) + (1,) * (entries.ndim - 1 - position))

    near = jax.random.permutation(key, blocks)[block_of(target)]
    far = (block_of(target) + blocks // 2) % blocks
    return jnp.where((block_of(source) == near) | (block_of(source) == far), factor * entries, entries)


def levels(own_key, dims, pieces, least, largest):
    loudness, own = 1.0, jax.random.fold_in(own_key, 6)
    for axis_at, blocks in pieces:
        draws = jnp.exp(jax.random.uniform(jax.random.fold_in(own, axis_at), (blocks,), jnp.float32, least / len(pieces), largest / len(pieces)))
        loudness = loudness * jnp.repeat(draws, dims[axis_at] // blocks).reshape([-1 if axis == axis_at else 1 for axis in range(len(dims))])
    return loudness


def gaussian(key, shape, width, bound, pieces=(), kind=jnp.bfloat16):
    drawn = width * jax.random.normal(key, shape, jnp.float32)
    if pieces:
        drawn = drawn * levels(key, shape, pieces, -0.22, 0.18)
    return jnp.clip(drawn, -bound, bound).astype(kind)


def bell_draw_with(rng, dims, spread, reach, pieces, heavy, held_as=jnp.bfloat16):
    values = spread * jax.random.normal(rng, dims, jnp.float32)
    if pieces:
        values = values * levels(rng, dims, pieces, -0.22, 0.18)
    return jnp.clip(spiked(values, jax.random.fold_in(rng, 3), *heavy), -reach, reach).astype(held_as)


def setup_inputs(seed: int = 0) -> dict:
    arg_keys = jax.random.split(jax.random.key(seed), 8)
    partial_grads = bell_draw_with(arg_keys[0], (N_DP, ROWS, FF), 1.0, 6.0, ((0, 16), (2, 8)), (0, 1, 16, 2.0))
    master = gaussian(arg_keys[1], (ROWS, FF), 1.0, 6.0, ((0, 128),), jnp.float32)
    first_moment = gaussian(arg_keys[2], (ROWS, FF), 0.5, 6.0, ((0, 128),), jnp.float32)
    second_moment = jnp.clip(jnp.exp(math.log(4.0) - 5.9914646 * jax.random.uniform(arg_keys[3], (ROWS, FF), jnp.float32) ** levels(arg_keys[3], (ROWS, FF), ((0, 128),), -0.2, 0.2)), 0.01, 4.0)
    noise_draws = gaussian(arg_keys[4], (HISTORY, ROWS, FF), 1.0, 6.0, ((1, 128),))
    band_coeffs = touch_ends(jax.random.randint(arg_keys[5], (HISTORY,), 1, 33), jax.random.fold_in(arg_keys[5], 1), 1, 32).astype(jnp.int32)
    step = jax.random.randint(arg_keys[6], (1,), 0, 16).astype(jnp.int32)
    return {"partial_grads": partial_grads, "master": master, "first_moment": first_moment, "second_moment": second_moment, "noise_draws": noise_draws, "band_coeffs": band_coeffs, "step": step}


def reference(partial_grads, master, first_moment, second_moment, noise_draws, band_coeffs, step):

    def add_replica(index, total):
        return total + partial_grads[index].astype(jnp.float32)
    grad_sum = lax.fori_loop(0, partial_grads.shape[0], add_replica, jnp.zeros(master.shape, jnp.float32))
    slots = jnp.arange(HISTORY, dtype=jnp.int32)
    lags = (step[0] - slots) % HISTORY
    onehot = (lags[:, None] == slots[None, :]).astype(jnp.float32)
    slot_weight = lax.optimization_barrier(jnp.sum(onehot * band_coeffs[None, :].astype(jnp.float32), axis=1)) / 32.0

    def add_slot(index, total):
        return total + slot_weight[index] * noise_draws[index].astype(jnp.float32)
    noise = lax.fori_loop(0, HISTORY, add_slot, jnp.zeros(master.shape, jnp.float32))
    gradient = 0.25 * (grad_sum + noise)
    new_first = 0.9 * first_moment + 0.1 * gradient
    new_second = 0.95 * second_moment + 0.05 * gradient * gradient
    count = (step[0] + 1).astype(jnp.float32)
    correct_one = 1.0 - jnp.power(jnp.float32(0.9), count)
    correct_two = 1.0 - jnp.power(jnp.float32(0.95), count)
    update = new_first / correct_one / (jnp.sqrt(new_second / correct_two) + 1e-08) + 0.1 * master
    new_master = master - 0.02 * update
    return (new_master, new_first, new_second, new_master.astype(jnp.bfloat16))
```

```python
import functools

import jax
import jax.numpy as jnp
from jax import lax
from jax.experimental import pallas as pl
from jax.experimental.pallas import tpu as pltpu
from jax.sharding import Mesh, PartitionSpec as P

HISTORY = 16
GROUP = ("z_hi", "x", "y", "z_lo")
DP = ("z_hi", "x", "core")
TENSOR = ("y", "z_lo")
SWAP = [(0, 1), (1, 0)]
VMEM_BYTES = 16 * 1024 * 1024


def noise_kernel(coeffs_ref, step_ref, draws_ref, noise_ref):
    total = None
    for slot in range(HISTORY):
        weight = coeffs_ref[(step_ref[0] - slot) & (HISTORY - 1)].astype(jnp.float32) / 32.0
        term = weight * draws_ref[slot].astype(jnp.float32)
        total = term if total is None else total + term
    noise_ref[...] = total


def noise_sum(band_coeffs, step, noise_draws, parts):
    slots, rows, columns = noise_draws.shape
    width = columns // parts
    return pl.pallas_call(
        noise_kernel,
        out_shape=jax.ShapeDtypeStruct((rows, columns), jnp.float32),
        grid=(parts,),
        in_specs=[
            pl.BlockSpec(memory_space=pltpu.SMEM),
            pl.BlockSpec(memory_space=pltpu.SMEM),
            pl.BlockSpec((slots, rows, width), lambda i: (0, 0, i)),
        ],
        out_specs=pl.BlockSpec((rows, width), lambda i: (0, i)),
        compiler_params=pltpu.CompilerParams(vmem_limit_bytes=VMEM_BYTES),
        cost_estimate=pl.CostEstimate(
            flops=2 * slots * rows * columns, bytes_accessed=2 * slots * rows * columns, transcendentals=0
        ),
        name="noise_sum",
    )(band_coeffs, step, noise_draws)


def adam_kernel(
    correct_ref, sums_ref, noise_ref, master_ref, first_ref, second_ref,
    new_master_ref, new_first_ref, new_second_ref, rounded_ref,
):
    sources, copies = sums_ref.shape[0], rounded_ref.shape[0]
    grad_sum = sums_ref[0, 0].astype(jnp.float32)
    for source in range(1, sources):
        grad_sum = grad_sum + sums_ref[source, 0].astype(jnp.float32)
    gradient = 0.25 * (grad_sum + noise_ref[...])
    new_first = 0.9 * first_ref[...] + 0.1 * gradient
    new_second = 0.95 * second_ref[...] + 0.05 * gradient * gradient
    master = master_ref[...]
    update = new_first / correct_ref[0] / (jnp.sqrt(new_second / correct_ref[1]) + 1e-08) + 0.1 * master
    new_master = master - 0.02 * update
    new_master_ref[...] = new_master
    new_first_ref[...] = new_first
    new_second_ref[...] = new_second
    rounded = new_master.astype(jnp.bfloat16)
    for copy in range(copies):
        rounded_ref[copy, 0] = rounded


def adam(correct, sums, noise, master, first, second):
    sources, parts, rows, width = sums.shape
    state = pl.BlockSpec((rows, width), lambda i: (0, i))
    spread = pl.BlockSpec((sources, 1, rows, width), lambda i: (0, i, 0, 0))
    whole = jax.ShapeDtypeStruct(master.shape, jnp.float32)
    return pl.pallas_call(
        adam_kernel,
        out_shape=(whole, whole, whole, jax.ShapeDtypeStruct(sums.shape, jnp.bfloat16)),
        grid=(parts,),
        in_specs=[pl.BlockSpec(memory_space=pltpu.SMEM), spread, state, state, state, state],
        out_specs=(state, state, state, spread),
        compiler_params=pltpu.CompilerParams(vmem_limit_bytes=VMEM_BYTES),
        name="adam",
    )(correct, sums, noise, master, first, second)


def place_kernel(side_ref, block_ref, *refs):
    out_ref, sem = refs[-2:]
    copy = pltpu.make_async_copy(block_ref, out_ref.at[:, side_ref[0]], sem)
    copy.start()
    copy.wait()


def place(block, side, into=None):
    chips, rows, columns = block.shape
    anywhere = pl.BlockSpec(memory_space=pl.ANY)
    more = () if into is None else (into,)
    return pl.pallas_call(
        place_kernel,
        out_shape=jax.ShapeDtypeStruct((chips, 2, rows, columns), block.dtype),
        in_specs=[pl.BlockSpec(memory_space=pltpu.SMEM), anywhere] + [anywhere] * len(more),
        out_specs=anywhere,
        scratch_shapes=[pltpu.SemaphoreType.DMA],
        input_output_aliases={2: 0} if more else {},
        compiler_params=pltpu.CompilerParams(vmem_limit_bytes=1024 * 1024),
        cost_estimate=pl.CostEstimate(flops=0, bytes_accessed=4 * block.size, transcendentals=0),
        name="place",
    )(side.reshape(1), block, *more)


def local(chips, tensors, partial_grads, master, first_moment, second_moment, noise_draws, band_coeffs, step):
    core = lax.axis_index("core")
    _, rows, width = partial_grads.shape
    own_rows = rows // (2 * chips * tensors)

    halves = partial_grads.reshape(chips, 2, rows // (2 * chips), width)
    given = lax.dynamic_index_in_dim(halves, 1 - core, 1, keepdims=False)
    kept = lax.dynamic_index_in_dim(halves, core, 1, keepdims=False)
    received = lax.ppermute(given, "core", SWAP)
    paired = (kept.astype(jnp.float32) + received.astype(jnp.float32)).astype(jnp.bfloat16)

    pieces = paired.reshape(chips * tensors, own_rows, width)
    sums = lax.all_to_all(pieces, GROUP, split_axis=0, concat_axis=0, tiled=True)
    sums = sums.reshape(chips, tensors, own_rows, width)

    noise = noise_sum(band_coeffs, step, noise_draws, tensors)
    count = (step[0] + 1).astype(jnp.float32)
    correct = 1.0 - jnp.power(jnp.array([0.9, 0.95], jnp.float32), count)
    new_master, new_first, new_second, spread = adam(
        correct, sums, noise, master, first_moment, second_moment
    )

    gathered = lax.all_to_all(
        spread.reshape(chips * tensors, own_rows, width), GROUP, split_axis=0, concat_axis=0, tiled=True
    ).reshape(chips, tensors * own_rows, width)
    other = lax.ppermute(gathered, "core", SWAP)
    weights = place(gathered, core)
    weights = place(other, 1 - core, weights)
    return (new_master, new_first, new_second, weights.reshape(rows, width))


def solution(mesh):
    fine = Mesh(mesh.devices.reshape(2, 4, 2, 4, 2), ("z_hi", "x", "core", "y", "z_lo"))
    owners = DP + TENSOR
    return jax.shard_map(
        functools.partial(local, 8, 8),
        mesh=fine,
        in_specs=(
            P(DP, None, TENSOR),
            P(owners, None),
            P(owners, None),
            P(owners, None),
            P(None, owners, None),
            P(),
            P(),
        ),
        out_specs=(P(owners, None), P(owners, None), P(owners, None), P(None, TENSOR)),
        check_vma=False,
    )
```

```python
import functools

import jax
import jax.numpy as jnp
from jax import lax
from jax.experimental import pallas as pl
from jax.experimental.pallas import tpu as pltpu
from jax.sharding import Mesh, PartitionSpec as P

HISTORY = 16
GROUP = ("z_hi", "x", "y", "z_lo")
DP = ("z_hi", "x", "core")
TENSOR = ("y", "z_lo")
Z, X, Y, T = 2, 4, 4, 8
VMEM_BYTES = 16 * 1024 * 1024
SMALL = 1024 * 1024
SMEM = pl.BlockSpec(memory_space=pltpu.SMEM)
ANY = pl.BlockSpec(memory_space=pl.ANY)
F32, BF16 = jnp.float32, jnp.bfloat16


def struct(shape, dtype):
    return jax.ShapeDtypeStruct(shape, dtype)


def in_hbm(array):
    return pltpu.with_memory_space_constraint(array, pltpu.HBM)


def in_vmem(array):
    return pltpu.with_memory_space_constraint(array, pltpu.VMEM)


def run_copies(copies, sems):
    started = [pltpu.make_async_copy(source, target, sems.at[i]) for i, (source, target) in enumerate(copies)]
    for copy in started:
        copy.start()
    for copy in started:
        copy.wait()


def copying(body, n, out_shape, n_in, aliases=None, moved=0, name=None):
    many = isinstance(out_shape, (tuple, list))

    def kernel(ids_ref, *refs):
        run_copies(body(ids_ref, refs[:n_in], refs[n_in:-1]), refs[-1])

    return pl.pallas_call(
        kernel,
        out_shape=out_shape,
        in_specs=[SMEM] + [ANY] * n_in,
        out_specs=[ANY] * len(out_shape) if many else ANY,
        scratch_shapes=[pltpu.SemaphoreType.DMA((n,))],
        input_output_aliases=aliases or {},
        compiler_params=pltpu.CompilerParams(vmem_limit_bytes=SMALL),
        cost_estimate=pl.CostEstimate(flops=0, bytes_accessed=moved, transcendentals=0),
        name=name,
    )


def split(ids, halves, other):
    chips, _, rows, columns = halves.shape

    def body(ids_ref, ins, outs):
        core = 1 - ids_ref[2] if other else ids_ref[2]
        return [(ins[0].at[i, core], outs[0].at[i]) for i in range(chips)]

    out = pltpu.VMEM((chips, rows, columns), BF16)
    name = "split_other" if other else "split_own"
    return copying(body, chips, [out], 1, moved=4 * chips * rows * columns, name=name)(ids, in_hbm(halves))[0]


def move(ids, arrays, space, name):
    def body(ids_ref, ins, outs):
        return list(zip(ins, outs))

    out = [space(a.shape, a.dtype) for a in arrays]
    moved = sum(2 * a.size * a.dtype.itemsize for a in arrays)
    return copying(body, len(arrays), out, len(arrays), moved=moved, name=name)(ids, *arrays)


def place(ids, block, other, into, name):
    chips, rows, columns = block.shape
    more = [] if into is None else [into]

    def body(ids_ref, ins, outs):
        core = 1 - ids_ref[2] if other else ids_ref[2]
        return [(ins[0].at[i], outs[0].at[i, core]) for i in range(chips)]

    out = struct((chips, 2, rows, columns), BF16)
    call = copying(body, chips, out, 1 + len(more), {2: 0} if more else {}, 4 * block.size, name)
    return call(ids, in_vmem(block), *more)


def noise_kernel(coeffs_ref, step_ref, draws_ref, noise_ref, held, sems):
    parts, width = held.shape[0], held.shape[-1]
    copies = [
        pltpu.make_async_copy(draws_ref.at[:, :, pl.ds(i * width, width)], held.at[i], sems.at[i])
        for i in range(parts)
    ]
    for copy in copies:
        copy.start()
    weights = [
        coeffs_ref[(step_ref[0] - slot) & (HISTORY - 1)].astype(F32) / 32.0 for slot in range(HISTORY)
    ]
    for i in range(parts):
        copies[i].wait()
        total = None
        for slot in range(HISTORY):
            term = weights[slot] * held[i, slot].astype(F32)
            total = term if total is None else total + term
        noise_ref[:, pl.ds(i * width, width)] = total


def noise_sum(band_coeffs, step, noise_draws):
    slots, rows, columns = noise_draws.shape
    return pl.pallas_call(
        noise_kernel,
        out_shape=[pltpu.VMEM((rows, columns), F32)],
        in_specs=[SMEM, SMEM, ANY],
        out_specs=[pl.BlockSpec(memory_space=pltpu.VMEM)],
        scratch_shapes=[
            pltpu.VMEM((T, slots, rows, columns // T), noise_draws.dtype), pltpu.SemaphoreType.DMA((T,)),
        ],
        compiler_params=pltpu.CompilerParams(vmem_limit_bytes=VMEM_BYTES),
        cost_estimate=pl.CostEstimate(
            flops=2 * slots * rows * columns, bytes_accessed=2 * slots * rows * columns, transcendentals=0
        ),
        name="noise_sum",
    )(band_coeffs, step, in_hbm(noise_draws))[0]


def adam(grad_sum, noise, master, first, second, correct_ref):
    gradient = 0.25 * (grad_sum + noise)
    new_first = 0.9 * first + 0.1 * gradient
    new_second = 0.95 * second + 0.05 * gradient * gradient
    update = new_first / correct_ref[0] / (jnp.sqrt(new_second / correct_ref[1]) + 1e-08) + 0.1 * master
    return master - 0.02 * update, new_first, new_second


def total_of(sums_ref):
    total = sums_ref[0, 0].astype(F32)
    for source in range(1, sums_ref.shape[0]):
        total = total + sums_ref[source, 0].astype(F32)
    return total


def adam_kernel(
    correct_ref, sums_ref, noise_ref, master_ref, first_ref, second_ref,
    new_master_ref, new_first_ref, new_second_ref, spread_ref,
):
    new_master, new_first_ref[...], new_second_ref[...] = adam(
        total_of(sums_ref), noise_ref[...], master_ref[...], first_ref[...], second_ref[...], correct_ref
    )
    new_master_ref[...] = new_master
    rounded = new_master.astype(BF16)
    for copy in range(spread_ref.shape[0]):
        spread_ref[copy, 0] = rounded


def adam_step(correct, sums, noise, master, first, second):
    sources, parts, rows, width = sums.shape
    state = pl.BlockSpec((rows, width), lambda i: (0, i))
    spread = pl.BlockSpec((sources, 1, rows, width), lambda i: (0, i, 0, 0))
    return pl.pallas_call(
        adam_kernel,
        out_shape=[pltpu.VMEM(master.shape, F32)] * 3 + [pltpu.VMEM(sums.shape, BF16)],
        grid=(parts,),
        in_specs=[SMEM, spread, state, state, state, state],
        out_specs=[state] * 3 + [spread],
        compiler_params=pltpu.CompilerParams(vmem_limit_bytes=VMEM_BYTES),
        name="adam_step",
    )(correct, in_vmem(sums), in_vmem(noise), in_vmem(master), in_vmem(first), in_vmem(second))


def swap(value, axis):
    return lax.ppermute(value, axis, [(0, 1), (1, 0)])


def plus_kernel(a_ref, b_ref, out_ref):
    out_ref[...] = (a_ref[...].astype(F32) + b_ref[...].astype(F32)).astype(BF16)


def plus(a, b):
    chips, rows, columns = a.shape
    block = pl.BlockSpec((1, rows, columns), lambda i: (i, 0, 0))
    return pl.pallas_call(
        plus_kernel,
        out_shape=[pltpu.VMEM(a.shape, BF16)],
        grid=(chips,),
        in_specs=[block, block],
        out_specs=[block],
        compiler_params=pltpu.CompilerParams(vmem_limit_bytes=VMEM_BYTES),
        name="plus",
    )(in_vmem(a), in_vmem(b))[0]


def local(partial_grads, master, first, second, noise_draws, band_coeffs, step):
    ids = jnp.stack([lax.axis_index(name) for name in ("z_hi", "x", "core", "y", "z_lo")]).astype(jnp.int32)
    _, rows, columns = partial_grads.shape
    block = rows // (2 * X * Z)
    own = block // T
    halves = partial_grads.reshape(Z * X, 2, block, columns)

    got = swap(split(ids, halves, True), "core")
    kept = split(ids, halves, False)

    noise = noise_sum(band_coeffs, step, noise_draws)
    count = (step[0] + 1).astype(F32)
    correct = 1.0 - jnp.power(jnp.array([0.9, 0.95], F32), count)

    pieces = plus(kept, got).reshape(Z * X * T, own, columns)
    pieces, noise, correct = lax.optimization_barrier((pieces, noise, correct))
    sums = lax.all_to_all(pieces, GROUP, split_axis=0, concat_axis=0, tiled=True).reshape(Z * X, T, own, columns)
    *states, spread = adam_step(correct, sums, noise, master, first, second)

    gathered = lax.all_to_all(
        spread.reshape(Z * X * T, own, columns), GROUP, split_axis=0, concat_axis=0, tiled=True
    ).reshape(Z * X, block, columns)
    gathered, states = lax.optimization_barrier((gathered, states))
    other = swap(gathered, "core")
    weights = place(ids, gathered, False, None, "place_own")
    new_master, new_first, new_second = move(ids, [in_vmem(a) for a in states], pltpu.HBM, "store_states")
    weights = place(ids, other, True, weights, "place_other")
    return (new_master, new_first, new_second, weights.reshape(rows, columns))


def solution(mesh):
    fine = Mesh(mesh.devices.reshape(Z, X, 2, Y, 2), ("z_hi", "x", "core", "y", "z_lo"))
    owners = DP + TENSOR
    return jax.shard_map(
        local,
        mesh=fine,
        in_specs=(
            P(DP, None, TENSOR),
            P(owners, None),
            P(owners, None),
            P(owners, None),
            P(None, owners, None),
            P(),
            P(),
        ),
        out_specs=(P(owners, None), P(owners, None), P(owners, None), P(None, TENSOR)),
        check_vma=False,
    )
```

```python
import functools

import jax
import jax.numpy as jnp
from jax import lax
from jax.experimental import pallas as pl
from jax.experimental.pallas import tpu as pltpu
from jax.sharding import Mesh, PartitionSpec as P

HISTORY = 16
GROUP = ("y", "z_lo", "z_hi", "x")
DP = ("z_hi", "x", "core")
TENSOR = ("y", "z_lo")
Z, X, Y, T = 2, 4, 4, 8
VMEM_BYTES = 16 * 1024 * 1024
SMALL = 1024 * 1024
SMEM = pl.BlockSpec(memory_space=pltpu.SMEM)
ANY = pl.BlockSpec(memory_space=pl.ANY)
F32, BF16 = jnp.float32, jnp.bfloat16


def struct(shape, dtype):
    return jax.ShapeDtypeStruct(shape, dtype)


def in_hbm(array):
    return pltpu.with_memory_space_constraint(array, pltpu.HBM)


def in_vmem(array):
    return pltpu.with_memory_space_constraint(array, pltpu.VMEM)


def run_copies(copies, sems):
    started = [pltpu.make_async_copy(source, target, sems.at[i]) for i, (source, target) in enumerate(copies)]
    for copy in started:
        copy.start()
    for copy in started:
        copy.wait()


def copying(body, n, out_shape, n_in, aliases=None, moved=0, name=None):
    many = isinstance(out_shape, (tuple, list))

    def kernel(ids_ref, *refs):
        run_copies(body(ids_ref, refs[:n_in], refs[n_in:-1]), refs[-1])

    return pl.pallas_call(
        kernel,
        out_shape=out_shape,
        in_specs=[SMEM] + [ANY] * n_in,
        out_specs=[ANY] * len(out_shape) if many else ANY,
        scratch_shapes=[pltpu.SemaphoreType.DMA((n,))],
        input_output_aliases=aliases or {},
        compiler_params=pltpu.CompilerParams(vmem_limit_bytes=SMALL),
        cost_estimate=pl.CostEstimate(flops=0, bytes_accessed=moved, transcendentals=0),
        name=name,
    )


def split(ids, halves, parts, name):
    rows, columns = halves.shape[2:]

    def body(ids_ref, ins, outs):
        core = ids_ref[2]
        return [
            (ins[0].at[pl.ds(first, n), 1 - core if other else core], outs[i])
            for i, (first, n, other) in enumerate(parts)
        ]

    out = [pltpu.VMEM((n, rows, columns), BF16) for _, n, _ in parts]
    moved = 4 * rows * columns * sum(n for _, n, _ in parts)
    return copying(body, len(parts), out, 1, moved=moved, name=name)(ids, in_hbm(halves))


def move(ids, arrays, space, name):
    def body(ids_ref, ins, outs):
        return list(zip(ins, outs))

    out = [space(a.shape, a.dtype) for a in arrays]
    moved = sum(2 * a.size * a.dtype.itemsize for a in arrays)
    return copying(body, len(arrays), out, len(arrays), moved=moved, name=name)(ids, *arrays)


def place(ids, pieces, other, into, name):
    owners, chips, rows, columns = pieces.shape
    more = [] if into is None else [into]

    def body(ids_ref, ins, outs):
        core = 1 - ids_ref[2] if other else ids_ref[2]
        return [(ins[0].at[:, i], outs[0].at[i, core]) for i in range(chips)]

    out = struct((chips, 2, owners, rows, columns), BF16)
    call = copying(body, chips, out, 1 + len(more), {2: 0} if more else {}, 4 * pieces.size, name)
    return call(ids, in_vmem(pieces), *more)


def noise_kernel(coeffs_ref, step_ref, draws_ref, noise_ref):
    total = None
    for slot in range(HISTORY):
        weight = coeffs_ref[(step_ref[0] - slot) & (HISTORY - 1)].astype(F32) / 32.0
        term = weight * draws_ref[slot].astype(F32)
        total = term if total is None else total + term
    noise_ref[...] = total


def noise_sum(band_coeffs, step, noise_draws):
    slots, rows, columns = noise_draws.shape
    width = columns // T
    return pl.pallas_call(
        noise_kernel,
        out_shape=[pltpu.VMEM((rows, columns), F32)],
        grid=(T,),
        in_specs=[SMEM, SMEM, pl.BlockSpec((slots, rows, width), lambda i: (0, 0, i))],
        out_specs=[pl.BlockSpec((rows, width), lambda i: (0, i))],
        compiler_params=pltpu.CompilerParams(vmem_limit_bytes=VMEM_BYTES),
        cost_estimate=pl.CostEstimate(
            flops=2 * slots * rows * columns, bytes_accessed=2 * slots * rows * columns, transcendentals=0
        ),
        name="noise_sum",
    )(band_coeffs, step, in_vmem(noise_draws))[0]


def adam(grad_sum, noise, master, first, second, correct_ref):
    gradient = 0.25 * (grad_sum + noise)
    new_first = 0.9 * first + 0.1 * gradient
    new_second = 0.95 * second + 0.05 * gradient * gradient
    update = new_first / correct_ref[0] / (jnp.sqrt(new_second / correct_ref[1]) + 1e-08) + 0.1 * master
    return master - 0.02 * update, new_first, new_second


def total_of(sums_ref):
    total = sums_ref[0, 0].astype(F32)
    for source in range(1, sums_ref.shape[1]):
        total = total + sums_ref[0, source].astype(F32)
    return total


def adam_kernel(
    correct_ref, sums_ref, noise_ref, master_ref, first_ref, second_ref,
    new_master_ref, new_first_ref, new_second_ref, spread_ref,
):
    new_master, new_first_ref[...], new_second_ref[...] = adam(
        total_of(sums_ref), noise_ref[...], master_ref[...], first_ref[...], second_ref[...], correct_ref
    )
    new_master_ref[...] = new_master
    rounded = new_master.astype(BF16)
    for copy in range(spread_ref.shape[1]):
        spread_ref[0, copy] = rounded


def adam_step(correct, sums, noise, master, first, second):
    parts, sources, rows, width = sums.shape
    state = pl.BlockSpec((rows, width), lambda i: (0, i))
    spread = pl.BlockSpec((1, sources, rows, width), lambda i: (i, 0, 0, 0))
    return pl.pallas_call(
        adam_kernel,
        out_shape=[pltpu.VMEM(master.shape, F32)] * 3 + [pltpu.VMEM(sums.shape, BF16)],
        grid=(parts,),
        in_specs=[SMEM, spread, state, state, state, state],
        out_specs=[state] * 3 + [spread],
        compiler_params=pltpu.CompilerParams(vmem_limit_bytes=VMEM_BYTES),
        name="adam_step",
    )(correct, in_vmem(sums), in_vmem(noise), in_vmem(master), in_vmem(first), in_vmem(second))


def swap(value, axis):
    return lax.ppermute(value, axis, [(0, 1), (1, 0)])


def plus_kernel(a_ref, b_ref, *refs):
    out_ref = refs[-1]
    owners, _, rows, _ = out_ref.shape
    for t in range(owners):
        cut = slice(t * rows, (t + 1) * rows)
        out_ref[t, 0] = (a_ref[0, cut].astype(F32) + b_ref[0, cut].astype(F32)).astype(BF16)


def plus(a, b, first, chips, into):
    n, rows, columns = a.shape
    block = pl.BlockSpec((1, rows, columns), lambda i: (i, 0, 0))
    more = [] if into is None else [into]
    return pl.pallas_call(
        plus_kernel,
        out_shape=[pltpu.VMEM((T, chips, rows // T, columns), BF16)],
        grid=(n,),
        in_specs=[block, block] + [ANY] * len(more),
        out_specs=[pl.BlockSpec((T, 1, rows // T, columns), lambda i: (0, first + i, 0, 0))],
        input_output_aliases={2: 0} if more else {},
        compiler_params=pltpu.CompilerParams(vmem_limit_bytes=VMEM_BYTES),
        name="plus",
    )(in_vmem(a), in_vmem(b), *more)[0]


def local(partial_grads, master, first, second, noise_draws, band_coeffs, step):
    ids = jnp.stack([lax.axis_index(name) for name in ("z_hi", "x", "core", "y", "z_lo")]).astype(jnp.int32)
    _, rows, columns = partial_grads.shape
    block = rows // (2 * X * Z)
    own = block // T
    halves = partial_grads.reshape(Z * X, 2, block, columns)

    chips = Z * X
    half = chips // 2
    (given_a,) = split(ids, halves, [(0, half, True)], "split_first")
    got_a = swap(given_a, "core")
    given_b, kept_a, kept_b = split(
        ids, halves, [(half, half, True), (0, half, False), (half, half, False)], "split_rest"
    )
    got_b = swap(given_b, "core")

    noise = noise_sum(band_coeffs, step, noise_draws)
    count = (step[0] + 1).astype(F32)
    correct = 1.0 - jnp.power(jnp.array([0.9, 0.95], F32), count)

    pieces = plus(kept_a, got_a, 0, chips, None)
    pieces = plus(kept_b, got_b, half, chips, pieces)
    pieces, noise, correct = lax.optimization_barrier((pieces, noise, correct))
    sums = lax.all_to_all(
        pieces.reshape(T * chips, own, columns), GROUP, split_axis=0, concat_axis=0, tiled=True
    ).reshape(T, chips, own, columns)
    *states, spread = adam_step(correct, sums, noise, master, first, second)

    gathered = lax.all_to_all(
        spread.reshape(T * chips, own, columns), GROUP, split_axis=0, concat_axis=0, tiled=True
    ).reshape(T, chips, own, columns)
    gathered, states = lax.optimization_barrier((gathered, states))
    other = swap(gathered, "core")
    weights = place(ids, gathered, False, None, "place_own")
    new_master, new_first, new_second = move(ids, [in_vmem(a) for a in states], pltpu.HBM, "store_states")
    weights = place(ids, other, True, weights, "place_other")
    return (new_master, new_first, new_second, weights.reshape(rows, columns))


def solution(mesh):
    fine = Mesh(mesh.devices.reshape(Z, X, 2, Y, 2), ("z_hi", "x", "core", "y", "z_lo"))
    owners = DP + TENSOR
    return jax.shard_map(
        local,
        mesh=fine,
        in_specs=(
            P(DP, None, TENSOR),
            P(owners, None),
            P(owners, None),
            P(owners, None),
            P(None, owners, None),
            P(),
            P(),
        ),
        out_specs=(P(owners, None), P(owners, None), P(owners, None), P(None, TENSOR)),
        check_vma=False,
    )
```

```python
import functools

import jax
import jax.numpy as jnp
from jax import lax
from jax.experimental import pallas as pl
from jax.experimental.pallas import tpu as pltpu
from jax.sharding import Mesh, PartitionSpec as P

HISTORY = 16
GROUP = ("y", "z_lo", "z_hi", "x")
DP = ("z_hi", "x", "core")
TENSOR = ("y", "z_lo")
Z, X, Y, T = 2, 4, 4, 8
EARLY = 5
VMEM_BYTES = 16 * 1024 * 1024
SMALL = 1024 * 1024
SMEM = pl.BlockSpec(memory_space=pltpu.SMEM)
ANY = pl.BlockSpec(memory_space=pl.ANY)
VMEM = pl.BlockSpec(memory_space=pltpu.VMEM)
F32, BF16 = jnp.float32, jnp.bfloat16


def struct(shape, dtype):
    return jax.ShapeDtypeStruct(shape, dtype)


def in_hbm(array):
    return pltpu.with_memory_space_constraint(array, pltpu.HBM)


def in_vmem(array):
    return pltpu.with_memory_space_constraint(array, pltpu.VMEM)


def run_copies(copies, sems):
    started = [pltpu.make_async_copy(source, target, sems.at[i]) for i, (source, target) in enumerate(copies)]
    for copy in started:
        copy.start()
    for copy in started:
        copy.wait()


def copying(body, n, out_shape, n_in, aliases=None, moved=0, name=None):
    many = isinstance(out_shape, (tuple, list))

    def kernel(ids_ref, *refs):
        run_copies(body(ids_ref, refs[:n_in], refs[n_in:-1]), refs[-1])

    return pl.pallas_call(
        kernel,
        out_shape=out_shape,
        in_specs=[SMEM] + [ANY] * n_in,
        out_specs=[ANY] * len(out_shape) if many else ANY,
        scratch_shapes=[pltpu.SemaphoreType.DMA((n,))],
        input_output_aliases=aliases or {},
        compiler_params=pltpu.CompilerParams(vmem_limit_bytes=SMALL),
        cost_estimate=pl.CostEstimate(flops=0, bytes_accessed=moved, transcendentals=0),
        name=name,
    )


def split(ids, halves, parts, name):
    rows, columns = halves.shape[2:]

    def body(ids_ref, ins, outs):
        core = ids_ref[2]
        return [
            (ins[0].at[pl.ds(first, n), 1 - core if other else core], outs[i])
            for i, (first, n, other) in enumerate(parts)
        ]

    out = [pltpu.VMEM((n, rows, columns), BF16) for _, n, _ in parts]
    moved = 4 * rows * columns * sum(n for _, n, _ in parts)
    return copying(body, len(parts), out, 1, moved=moved, name=name)(ids, in_hbm(halves))


def place_own(ids, pieces, states):
    owners, chips, rows, columns = pieces.shape

    def body(ids_ref, ins, outs):
        copies = [(ins[0].at[:, i], outs[0].at[i, ids_ref[2]]) for i in range(chips)]
        return copies + list(zip(ins[1:], outs[1:]))

    out = [pltpu.HBM((chips, 2, owners, rows, columns), BF16)] + [pltpu.HBM(a.shape, a.dtype) for a in states]
    moved = 4 * pieces.size + sum(8 * a.size for a in states)
    call = copying(body, chips + len(states), out, 1 + len(states), moved=moved, name="place_own")
    return call(ids, *[in_vmem(a) for a in (pieces, *states)])


def place_other(ids, pieces, first, into, name):
    n = pieces.shape[0]

    def body(ids_ref, ins, outs):
        return [(ins[0].at[t], outs[0].at[:, 1 - ids_ref[2], first + t]) for t in range(n)]

    call = copying(body, n, struct(into.shape, BF16), 2, {2: 0}, 4 * pieces.size, name)
    return call(ids, in_vmem(pieces), into)


def noise_kernel(coeffs_ref, step_ref, draws_ref, noise_ref):
    weights = [
        coeffs_ref[(step_ref[0] - slot) & (HISTORY - 1)].astype(F32) / 32.0 for slot in range(HISTORY)
    ]
    width = 3584

    def part(i, carry):
        cut = pl.ds(pl.multiple_of(i * width, width), width)
        total = None
        for slot in range(HISTORY):
            term = weights[slot] * draws_ref[slot, :, cut].astype(F32)
            total = term if total is None else total + term
        noise_ref[:, cut] = total
        return carry

    lax.fori_loop(0, noise_ref.shape[1] // width, part, 0)


def noise_sum(band_coeffs, step, noise_draws):
    slots, rows, columns = noise_draws.shape
    return pl.pallas_call(
        noise_kernel,
        out_shape=[pltpu.VMEM((rows, columns), F32)],
        in_specs=[SMEM, SMEM, VMEM],
        out_specs=[VMEM],
        compiler_params=pltpu.CompilerParams(vmem_limit_bytes=VMEM_BYTES),
        cost_estimate=pl.CostEstimate(
            flops=2 * slots * rows * columns, bytes_accessed=2 * slots * rows * columns, transcendentals=0
        ),
        name="noise_sum",
    )(band_coeffs, step, in_vmem(noise_draws))[0]


def adam(grad_sum, noise, master, first, second, correct_ref):
    gradient = 0.25 * (grad_sum + noise)
    new_first = 0.9 * first + 0.1 * gradient
    new_second = 0.95 * second + 0.05 * gradient * gradient
    update = new_first / correct_ref[0] / (jnp.sqrt(new_second / correct_ref[1]) + 1e-08) + 0.1 * master
    return master - 0.02 * update, new_first, new_second


def total_of(sums_ref):
    total = sums_ref[0, 0].astype(F32)
    for source in range(1, sums_ref.shape[1]):
        total = total + sums_ref[0, source].astype(F32)
    return total


def adam_kernel(
    correct_ref, sums_ref, noise_ref, master_ref, first_ref, second_ref,
    new_master_ref, new_first_ref, new_second_ref, spread_ref,
):
    new_master, new_first_ref[...], new_second_ref[...] = adam(
        total_of(sums_ref), noise_ref[...], master_ref[...], first_ref[...], second_ref[...], correct_ref
    )
    new_master_ref[...] = new_master
    rounded = new_master.astype(BF16)
    for copy in range(spread_ref.shape[1]):
        spread_ref[0, copy] = rounded


def adam_step(correct, sums, noise, master, first, second):
    parts, sources, rows, width = sums.shape
    state = pl.BlockSpec((rows, width), lambda i: (0, i))
    spread = pl.BlockSpec((1, sources, rows, width), lambda i: (i, 0, 0, 0))
    return pl.pallas_call(
        adam_kernel,
        out_shape=[pltpu.VMEM(master.shape, F32)] * 3 + [pltpu.VMEM(sums.shape, BF16)],
        grid=(parts,),
        in_specs=[SMEM, spread, state, state, state, state],
        out_specs=[state] * 3 + [spread],
        compiler_params=pltpu.CompilerParams(vmem_limit_bytes=VMEM_BYTES),
        name="adam_step",
    )(correct, in_vmem(sums), in_vmem(noise), in_vmem(master), in_vmem(first), in_vmem(second))


def swap(value, axis):
    return lax.ppermute(value, axis, [(0, 1), (1, 0)])


def plus_kernel(a_ref, b_ref, *refs):
    out_ref = refs[-1]
    owners, _, rows, _ = out_ref.shape
    for t in range(owners):
        cut = slice(t * rows, (t + 1) * rows)
        out_ref[t, 0] = (a_ref[0, cut].astype(F32) + b_ref[0, cut].astype(F32)).astype(BF16)


def plus(a, b, first, chips, into):
    n, rows, columns = a.shape
    block = pl.BlockSpec((1, rows, columns), lambda i: (i, 0, 0))
    more = [] if into is None else [into]
    return pl.pallas_call(
        plus_kernel,
        out_shape=[pltpu.VMEM((T, chips, rows // T, columns), BF16)],
        grid=(n,),
        in_specs=[block, block] + [ANY] * len(more),
        out_specs=[pl.BlockSpec((T, 1, rows // T, columns), lambda i: (0, first + i, 0, 0))],
        input_output_aliases={2: 0} if more else {},
        compiler_params=pltpu.CompilerParams(vmem_limit_bytes=VMEM_BYTES),
        name="plus",
    )(in_vmem(a), in_vmem(b), *more)[0]


def local(partial_grads, master, first, second, noise_draws, band_coeffs, step):
    ids = jnp.stack([lax.axis_index(name) for name in ("z_hi", "x", "core", "y", "z_lo")]).astype(jnp.int32)
    _, rows, columns = partial_grads.shape
    block = rows // (2 * X * Z)
    own = block // T
    halves = partial_grads.reshape(Z * X, 2, block, columns)

    chips = Z * X
    half = chips // 2
    (given_a,) = split(ids, halves, [(0, half, True)], "split_first")
    got_a = swap(given_a, "core")
    given_b, kept_a, kept_b = split(
        ids, halves, [(half, half, True), (0, half, False), (half, half, False)], "split_rest"
    )
    got_b = swap(given_b, "core")

    noise = noise_sum(band_coeffs, step, noise_draws)
    count = (step[0] + 1).astype(F32)
    correct = 1.0 - jnp.power(jnp.array([0.9, 0.95], F32), count)

    pieces = plus(kept_a, got_a, 0, chips, None)
    pieces = plus(kept_b, got_b, half, chips, pieces)
    pieces, noise, correct = lax.optimization_barrier((pieces, noise, correct))
    sums = lax.all_to_all(
        pieces.reshape(T * chips, own, columns), GROUP, split_axis=0, concat_axis=0, tiled=True
    ).reshape(T, chips, own, columns)
    *states, spread = adam_step(correct, sums, noise, master, first, second)

    gathered = lax.all_to_all(
        spread.reshape(T * chips, own, columns), GROUP, split_axis=0, concat_axis=0, tiled=True
    ).reshape(T, chips, own, columns)
    gathered, states = lax.optimization_barrier((gathered, states))
    other_a = swap(gathered[:EARLY], "core")
    other_b = swap(gathered[EARLY:], "core")
    weights, new_master, new_first, new_second = place_own(ids, gathered, states)
    weights = place_other(ids, other_a, 0, weights, "place_early")
    weights = place_other(ids, other_b, EARLY, weights, "place_late")
    return (new_master, new_first, new_second, weights.reshape(rows, columns))


def solution(mesh):
    fine = Mesh(mesh.devices.reshape(Z, X, 2, Y, 2), ("z_hi", "x", "core", "y", "z_lo"))
    owners = DP + TENSOR
    return jax.shard_map(
        local,
        mesh=fine,
        in_specs=(
            P(DP, None, TENSOR),
            P(owners, None),
            P(owners, None),
            P(owners, None),
            P(None, owners, None),
            P(),
            P(),
        ),
        out_specs=(P(owners, None), P(owners, None), P(owners, None), P(None, TENSOR)),
        check_vma=False,
    )
```

```python
import functools

import jax
import jax.numpy as jnp
from jax import lax
from jax.experimental import pallas as pl
from jax.experimental.pallas import tpu as pltpu
from jax.sharding import Mesh, PartitionSpec as P

HISTORY = 16
GROUP = ("y", "z_lo", "z_hi", "x")
DP = ("z_hi", "x", "core")
TENSOR = ("y", "z_lo")
Z, X, Y, T = 2, 4, 4, 8
EARLY = 5
VMEM_BYTES = 16 * 1024 * 1024
SMALL = 1024 * 1024
SMEM = pl.BlockSpec(memory_space=pltpu.SMEM)
ANY = pl.BlockSpec(memory_space=pl.ANY)
VMEM = pl.BlockSpec(memory_space=pltpu.VMEM)
F32, BF16 = jnp.float32, jnp.bfloat16


def struct(shape, dtype):
    return jax.ShapeDtypeStruct(shape, dtype)


def in_hbm(array):
    return pltpu.with_memory_space_constraint(array, pltpu.HBM)


def in_vmem(array):
    return pltpu.with_memory_space_constraint(array, pltpu.VMEM)


def run_copies(copies, sems):
    started = [pltpu.make_async_copy(source, target, sems.at[i]) for i, (source, target) in enumerate(copies)]
    for copy in started:
        copy.start()
    for copy in started:
        copy.wait()


def copying(body, n, out_shape, n_in, aliases=None, moved=0, name=None):
    many = isinstance(out_shape, (tuple, list))

    def kernel(ids_ref, *refs):
        run_copies(body(ids_ref, refs[:n_in], refs[n_in:-1]), refs[-1])

    return pl.pallas_call(
        kernel,
        out_shape=out_shape,
        in_specs=[SMEM] + [ANY] * n_in,
        out_specs=[ANY] * len(out_shape) if many else ANY,
        scratch_shapes=[pltpu.SemaphoreType.DMA((n,))],
        input_output_aliases=aliases or {},
        compiler_params=pltpu.CompilerParams(vmem_limit_bytes=SMALL),
        cost_estimate=pl.CostEstimate(flops=0, bytes_accessed=moved, transcendentals=0),
        name=name,
    )


def split(ids, halves, parts, name):
    rows, columns = halves.shape[2:]

    def body(ids_ref, ins, outs):
        core = ids_ref[2]
        return [
            (ins[0].at[pl.ds(first, n), 1 - core if other else core], outs[i])
            for i, (first, n, other) in enumerate(parts)
        ]

    out = [pltpu.VMEM((n, rows, columns), BF16) for _, n, _ in parts]
    moved = 4 * rows * columns * sum(n for _, n, _ in parts)
    return copying(body, len(parts), out, 1, moved=moved, name=name)(ids, in_hbm(halves))


def place_own(ids, pieces, states):
    owners, chips, rows, columns = pieces.shape

    def body(ids_ref, ins, outs):
        copies = [(ins[0].at[:, i], outs[0].at[i, ids_ref[2]]) for i in range(chips)]
        return copies + list(zip(ins[1:], outs[1:]))

    out = [pltpu.HBM((chips, 2, owners, rows, columns), BF16)] + [pltpu.HBM(a.shape, a.dtype) for a in states]
    moved = 4 * pieces.size + sum(8 * a.size for a in states)
    call = copying(body, chips + len(states), out, 1 + len(states), moved=moved, name="place_own")
    return call(ids, *[in_vmem(a) for a in (pieces, *states)])


def place_other(ids, pieces, first, into, name):
    n = pieces.shape[0]

    def body(ids_ref, ins, outs):
        return [(ins[0].at[t], outs[0].at[:, 1 - ids_ref[2], first + t]) for t in range(n)]

    call = copying(body, n, struct(into.shape, BF16), 2, {2: 0}, 4 * pieces.size, name)
    return call(ids, in_vmem(pieces), into)


def noise_kernel(coeffs_ref, step_ref, draws_ref, noise_ref):
    weights = [
        coeffs_ref[(step_ref[0] - slot) & (HISTORY - 1)].astype(F32) / 32.0 for slot in range(HISTORY)
    ]
    width = 3584

    def part(i, carry):
        cut = pl.ds(pl.multiple_of(i * width, width), width)
        total = None
        for slot in range(HISTORY):
            term = weights[slot] * draws_ref[slot, :, cut].astype(F32)
            total = term if total is None else total + term
        noise_ref[:, cut] = total
        return carry

    lax.fori_loop(0, noise_ref.shape[1] // width, part, 0)


def noise_sum(band_coeffs, step, noise_draws):
    slots, rows, columns = noise_draws.shape
    return pl.pallas_call(
        noise_kernel,
        out_shape=[pltpu.VMEM((rows, columns), F32)],
        in_specs=[SMEM, SMEM, VMEM],
        out_specs=[VMEM],
        compiler_params=pltpu.CompilerParams(vmem_limit_bytes=VMEM_BYTES),
        cost_estimate=pl.CostEstimate(
            flops=2 * slots * rows * columns, bytes_accessed=2 * slots * rows * columns, transcendentals=0
        ),
        name="noise_sum",
    )(band_coeffs, step, in_vmem(noise_draws))[0]


def adam(grad_sum, noise, master, first, second, correct_ref):
    gradient = 0.25 * (grad_sum + noise)
    new_first = 0.9 * first + 0.1 * gradient
    new_second = 0.95 * second + 0.05 * gradient * gradient
    update = new_first / correct_ref[0] / (jnp.sqrt(new_second / correct_ref[1]) + 1e-08) + 0.1 * master
    return master - 0.02 * update, new_first, new_second


def total_of(sums_ref):
    total = sums_ref[0, 0].astype(F32)
    for source in range(1, sums_ref.shape[1]):
        total = total + sums_ref[0, source].astype(F32)
    return total


def adam_kernel(
    correct_ref, sums_ref, noise_ref, master_ref, first_ref, second_ref,
    new_master_ref, new_first_ref, new_second_ref, spread_ref,
):
    new_master, new_first_ref[...], new_second_ref[...] = adam(
        total_of(sums_ref), noise_ref[...], master_ref[...], first_ref[...], second_ref[...], correct_ref
    )
    new_master_ref[...] = new_master
    rounded = new_master.astype(BF16)
    for copy in range(spread_ref.shape[1]):
        spread_ref[0, copy] = rounded


def adam_step(correct, sums, noise, master, first, second):
    parts, sources, rows, width = sums.shape
    state = pl.BlockSpec((rows, width), lambda i: (0, i))
    spread = pl.BlockSpec((1, sources, rows, width), lambda i: (i, 0, 0, 0))
    return pl.pallas_call(
        adam_kernel,
        out_shape=[pltpu.VMEM(master.shape, F32)] * 3 + [pltpu.VMEM(sums.shape, BF16)],
        grid=(parts,),
        in_specs=[SMEM, spread, state, state, state, state],
        out_specs=[state] * 3 + [spread],
        compiler_params=pltpu.CompilerParams(vmem_limit_bytes=VMEM_BYTES),
        name="adam_step",
    )(correct, in_vmem(sums), in_vmem(noise), in_vmem(master), in_vmem(first), in_vmem(second))


def swap(value, axis):
    return lax.ppermute(value, axis, [(0, 1), (1, 0)])


def plus_kernel(n_ids, *refs):
    a_ref, b_ref, out_ref = refs[n_ids], refs[n_ids + 1], refs[-1]
    owners, _, rows, _ = out_ref.shape
    for t in range(owners):
        cut = slice(t * rows, (t + 1) * rows)
        out_ref[t, 0] = (a_ref[0, cut].astype(F32) + b_ref[0, cut].astype(F32)).astype(BF16)


def plus(a, b, first, chips, into=None, ids=None):
    n, rows, columns = a.shape
    block = pl.BlockSpec((1, rows, columns), lambda i: (i, 0, 0))
    more = [] if into is None else [into]
    wait = [] if ids is None else [ids]
    return pl.pallas_call(
        functools.partial(plus_kernel, len(wait)),
        out_shape=[pltpu.VMEM((T, chips, rows // T, columns), BF16)],
        grid=(n,),
        in_specs=[SMEM] * len(wait) + [block, block] + [ANY] * len(more),
        out_specs=[pl.BlockSpec((T, 1, rows // T, columns), lambda i: (0, first + i, 0, 0))],
        input_output_aliases={len(wait) + 2: 0} if more else {},
        compiler_params=pltpu.CompilerParams(vmem_limit_bytes=VMEM_BYTES),
        name="plus",
    )(*wait, in_vmem(a), in_vmem(b), *more)[0]


TURN = (("z_hi", "x", "y"), ("x", "y"))
MESH = ("z_hi", "x", "core", "y", "z_lo")
SIZES = {"z_hi": Z, "x": X, "core": 2, "y": Y, "z_lo": 2}


def index_of(place):
    index = 0
    for name in MESH:
        index = index * SIZES[name] + place[name]
    return index


def after_turn(ids, ready):
    token = ids.astype(F32) + 0.0 * ready.reshape(-1)[: ids.shape[0]].astype(F32)
    for axes in TURN:
        pairs = []
        for flat in range(2 * X * Z * T):
            place, rest = {}, flat
            for name in reversed(MESH):
                place[name], rest = rest % SIZES[name], rest // SIZES[name]
            if place["core"] == 1:
                across = dict(place, **{a: (place[a] + SIZES[a] // 2) % SIZES[a] for a in axes})
                pairs.append((flat, index_of(across)))
        token = lax.ppermute(token, MESH, pairs)
    return ids + (token < 0.0).astype(jnp.int32)


def local(partial_grads, master, first, second, noise_draws, band_coeffs, step):
    ids = jnp.stack([lax.axis_index(name) for name in ("z_hi", "x", "core", "y", "z_lo")]).astype(jnp.int32)
    _, rows, columns = partial_grads.shape
    block = rows // (2 * X * Z)
    own = block // T
    halves = partial_grads.reshape(Z * X, 2, block, columns)

    chips = Z * X
    half = chips // 2
    (given_a,) = split(ids, halves, [(0, half, True)], "split_first")
    got_a = swap(given_a, "core")
    given_b, kept_a, kept_b = split(
        ids, halves, [(half, half, True), (0, half, False), (half, half, False)], "split_rest"
    )
    got_b = swap(given_b, "core")

    noise = noise_sum(band_coeffs, step, noise_draws)
    count = (step[0] + 1).astype(F32)
    correct = 1.0 - jnp.power(jnp.array([0.9, 0.95], F32), count)

    pieces = plus(kept_a, got_a, 0, chips)
    pieces = plus(kept_b, got_b, half, chips, pieces, after_turn(ids, got_a[0, 0, :8]))
    pieces, noise, correct = lax.optimization_barrier((pieces, noise, correct))
    sums = lax.all_to_all(
        pieces.reshape(T * chips, own, columns), GROUP, split_axis=0, concat_axis=0, tiled=True
    ).reshape(T, chips, own, columns)
    *states, spread = adam_step(correct, sums, noise, master, first, second)

    gathered = lax.all_to_all(
        spread.reshape(T * chips, own, columns), GROUP, split_axis=0, concat_axis=0, tiled=True
    ).reshape(T, chips, own, columns)
    gathered, states = lax.optimization_barrier((gathered, states))
    other_a = swap(gathered[:EARLY], "core")
    other_b = swap(gathered[EARLY:], "core")
    weights, new_master, new_first, new_second = place_own(ids, gathered, states)
    weights = place_other(ids, other_a, 0, weights, "place_early")
    weights = place_other(ids, other_b, EARLY, weights, "place_late")
    return (new_master, new_first, new_second, weights.reshape(rows, columns))


def solution(mesh):
    fine = Mesh(mesh.devices.reshape(Z, X, 2, Y, 2), ("z_hi", "x", "core", "y", "z_lo"))
    owners = DP + TENSOR
    return jax.shard_map(
        local,
        mesh=fine,
        in_specs=(
            P(DP, None, TENSOR),
            P(owners, None),
            P(owners, None),
            P(owners, None),
            P(None, owners, None),
            P(),
            P(),
        ),
        out_specs=(P(owners, None), P(owners, None), P(owners, None), P(None, TENSOR)),
        check_vma=False,
    )
```

```python
import functools

import jax
import jax.numpy as jnp
from jax import lax
from jax.experimental import pallas as pl
from jax.experimental.pallas import tpu as pltpu
from jax.sharding import Mesh, PartitionSpec as P

HISTORY = 16
GROUP = ("y", "z_lo", "z_hi", "x")
DP = ("z_hi", "x", "core")
TENSOR = ("y", "z_lo")
Z, X, Y, T = 2, 4, 4, 8
EARLY = 5
VMEM_BYTES = 16 * 1024 * 1024
SMALL = 1024 * 1024
SMEM = pl.BlockSpec(memory_space=pltpu.SMEM)
ANY = pl.BlockSpec(memory_space=pl.ANY)
VMEM = pl.BlockSpec(memory_space=pltpu.VMEM)
F32, BF16 = jnp.float32, jnp.bfloat16


def struct(shape, dtype):
    return jax.ShapeDtypeStruct(shape, dtype)


def in_hbm(array):
    return pltpu.with_memory_space_constraint(array, pltpu.HBM)


def in_vmem(array):
    return pltpu.with_memory_space_constraint(array, pltpu.VMEM)


def run_copies(copies, sems):
    started = [pltpu.make_async_copy(source, target, sems.at[i]) for i, (source, target) in enumerate(copies)]
    for copy in started:
        copy.start()
    for copy in started:
        copy.wait()


def copying(body, n, out_shape, n_in, aliases=None, moved=0, name=None):
    many = isinstance(out_shape, (tuple, list))

    def kernel(ids_ref, *refs):
        run_copies(body(ids_ref, refs[:n_in], refs[n_in:-1]), refs[-1])

    return pl.pallas_call(
        kernel,
        out_shape=out_shape,
        in_specs=[SMEM] + [ANY] * n_in,
        out_specs=[ANY] * len(out_shape) if many else ANY,
        scratch_shapes=[pltpu.SemaphoreType.DMA((n,))],
        input_output_aliases=aliases or {},
        compiler_params=pltpu.CompilerParams(vmem_limit_bytes=SMALL),
        cost_estimate=pl.CostEstimate(flops=0, bytes_accessed=moved, transcendentals=0),
        name=name,
    )


def split(ids, halves, parts, name):
    rows, columns = halves.shape[2:]

    def body(ids_ref, ins, outs):
        core = ids_ref[2]
        return [
            (ins[0].at[pl.ds(first, n), 1 - core if other else core], outs[i])
            for i, (first, n, other) in enumerate(parts)
        ]

    out = [pltpu.VMEM((n, rows, columns), BF16) for _, n, _ in parts]
    moved = 4 * rows * columns * sum(n for _, n, _ in parts)
    return copying(body, len(parts), out, 1, moved=moved, name=name)(ids, in_hbm(halves))


def place_own(ids, pieces, states):
    owners, chips, rows, columns = pieces.shape

    def body(ids_ref, ins, outs):
        copies = [(ins[0].at[:, i], outs[0].at[i, ids_ref[2]]) for i in range(chips)]
        return copies + list(zip(ins[1:], outs[1:]))

    out = [pltpu.HBM((chips, 2, owners, rows, columns), BF16)] + [pltpu.HBM(a.shape, a.dtype) for a in states]
    moved = 4 * pieces.size + sum(8 * a.size for a in states)
    call = copying(body, chips + len(states), out, 1 + len(states), moved=moved, name="place_own")
    return call(ids, *[in_vmem(a) for a in (pieces, *states)])


def place_other(ids, pieces, first, into, name):
    n = pieces.shape[0]

    def body(ids_ref, ins, outs):
        return [(ins[0].at[t], outs[0].at[:, 1 - ids_ref[2], first + t]) for t in range(n)]

    call = copying(body, n, struct(into.shape, BF16), 2, {2: 0}, 4 * pieces.size, name)
    return call(ids, in_vmem(pieces), into)


def noise_kernel(coeffs_ref, step_ref, draws_ref, noise_ref):
    weights = [
        coeffs_ref[(step_ref[0] - slot) & (HISTORY - 1)].astype(F32) / 32.0 for slot in range(HISTORY)
    ]
    width = 3584

    def part(i, carry):
        cut = pl.ds(pl.multiple_of(i * width, width), width)
        total = None
        for slot in range(HISTORY):
            term = weights[slot] * draws_ref[slot, :, cut].astype(F32)
            total = term if total is None else total + term
        noise_ref[:, cut] = total
        return carry

    lax.fori_loop(0, noise_ref.shape[1] // width, part, 0)


def noise_sum(band_coeffs, step, noise_draws):
    slots, rows, columns = noise_draws.shape
    return pl.pallas_call(
        noise_kernel,
        out_shape=[pltpu.VMEM((rows, columns), F32)],
        in_specs=[SMEM, SMEM, VMEM],
        out_specs=[VMEM],
        compiler_params=pltpu.CompilerParams(vmem_limit_bytes=VMEM_BYTES),
        cost_estimate=pl.CostEstimate(
            flops=2 * slots * rows * columns, bytes_accessed=2 * slots * rows * columns, transcendentals=0
        ),
        name="noise_sum",
    )(band_coeffs, step, in_vmem(noise_draws))[0]


def adam(grad_sum, noise, master, first, second, correct_ref):
    gradient = 0.25 * (grad_sum + noise)
    new_first = 0.9 * first + 0.1 * gradient
    new_second = 0.95 * second + 0.05 * gradient * gradient
    update = new_first / correct_ref[0] / (jnp.sqrt(new_second / correct_ref[1]) + 1e-08) + 0.1 * master
    return master - 0.02 * update, new_first, new_second


def total_of(sums_ref):
    total = sums_ref[0, 0].astype(F32)
    for source in range(1, sums_ref.shape[1]):
        total = total + sums_ref[0, source].astype(F32)
    return total


def adam_kernel(
    correct_ref, sums_ref, noise_ref, master_ref, first_ref, second_ref,
    new_master_ref, new_first_ref, new_second_ref, spread_ref,
):
    new_master, new_first_ref[...], new_second_ref[...] = adam(
        total_of(sums_ref), noise_ref[...], master_ref[...], first_ref[...], second_ref[...], correct_ref
    )
    new_master_ref[...] = new_master
    rounded = new_master.astype(BF16)
    for copy in range(spread_ref.shape[1]):
        spread_ref[0, copy] = rounded


def adam_step(correct, sums, noise, master, first, second):
    parts, sources, rows, width = sums.shape
    state = pl.BlockSpec((rows, width), lambda i: (0, i))
    spread = pl.BlockSpec((1, sources, rows, width), lambda i: (i, 0, 0, 0))
    return pl.pallas_call(
        adam_kernel,
        out_shape=[pltpu.VMEM(master.shape, F32)] * 3 + [pltpu.VMEM(sums.shape, BF16)],
        grid=(parts,),
        in_specs=[SMEM, spread, state, state, state, state],
        out_specs=[state] * 3 + [spread],
        compiler_params=pltpu.CompilerParams(vmem_limit_bytes=VMEM_BYTES),
        name="adam_step",
    )(correct, in_vmem(sums), in_vmem(noise), in_vmem(master), in_vmem(first), in_vmem(second))


def swap(value, axis):
    return lax.ppermute(value, axis, [(0, 1), (1, 0)])


def plus_kernel(n_ids, *refs):
    a_ref, b_ref, out_ref = refs[n_ids], refs[n_ids + 1], refs[-1]
    owners, _, rows, _ = out_ref.shape
    for t in range(owners):
        cut = slice(t * rows, (t + 1) * rows)
        out_ref[t, 0] = (a_ref[0, cut].astype(F32) + b_ref[0, cut].astype(F32)).astype(BF16)


def plus(a, b, first, chips, into=None, ids=None):
    n, rows, columns = a.shape
    block = pl.BlockSpec((1, rows, columns), lambda i: (i, 0, 0))
    more = [] if into is None else [into]
    wait = [] if ids is None else [ids]
    return pl.pallas_call(
        functools.partial(plus_kernel, len(wait)),
        out_shape=[pltpu.VMEM((T, chips, rows // T, columns), BF16)],
        grid=(n,),
        in_specs=[SMEM] * len(wait) + [block, block] + [ANY] * len(more),
        out_specs=[pl.BlockSpec((T, 1, rows // T, columns), lambda i: (0, first + i, 0, 0))],
        input_output_aliases={len(wait) + 2: 0} if more else {},
        compiler_params=pltpu.CompilerParams(vmem_limit_bytes=VMEM_BYTES),
        name="plus",
    )(*wait, in_vmem(a), in_vmem(b), *more)[0]


TURN = (("z_hi", "x", "y"), ("x", "y", "z_lo"))
MESH = ("z_hi", "x", "core", "y", "z_lo")
SIZES = {"z_hi": Z, "x": X, "core": 2, "y": Y, "z_lo": 2}


def index_of(place):
    index = 0
    for name in MESH:
        index = index * SIZES[name] + place[name]
    return index


def after_turn(ids, ready):
    token = ids.astype(F32) + 0.0 * ready.reshape(-1)[: ids.shape[0]].astype(F32)
    for axes in TURN:
        pairs = []
        for flat in range(2 * X * Z * T):
            place, rest = {}, flat
            for name in reversed(MESH):
                place[name], rest = rest % SIZES[name], rest // SIZES[name]
            if place["core"] == 1:
                across = dict(place, **{a: (place[a] + SIZES[a] // 2) % SIZES[a] for a in axes})
                pairs.append((flat, index_of(across)))
        token = lax.ppermute(token, MESH, pairs)
    return ids + (token < 0.0).astype(jnp.int32)


def local(partial_grads, master, first, second, noise_draws, band_coeffs, step):
    ids = jnp.stack([lax.axis_index(name) for name in ("z_hi", "x", "core", "y", "z_lo")]).astype(jnp.int32)
    _, rows, columns = partial_grads.shape
    block = rows // (2 * X * Z)
    own = block // T
    halves = partial_grads.reshape(Z * X, 2, block, columns)

    chips = Z * X
    half = chips // 2
    (given_a,) = split(ids, halves, [(0, half, True)], "split_first")
    got_a = swap(given_a, "core")
    given_b, kept_a, kept_b = split(
        ids, halves, [(half, half, True), (0, half, False), (half, half, False)], "split_rest"
    )
    got_b = swap(given_b, "core")

    noise = noise_sum(band_coeffs, step, noise_draws)
    count = (step[0] + 1).astype(F32)
    correct = 1.0 - jnp.power(jnp.array([0.9, 0.95], F32), count)

    pieces = plus(kept_a, got_a, 0, chips)
    pieces = plus(kept_b, got_b, half, chips, pieces, after_turn(ids, got_a[0, 0, :8]))
    pieces, noise, correct = lax.optimization_barrier((pieces, noise, correct))
    sums = lax.all_to_all(
        pieces.reshape(T * chips, own, columns), GROUP, split_axis=0, concat_axis=0, tiled=True
    ).reshape(T, chips, own, columns)
    *states, spread = adam_step(correct, sums, noise, master, first, second)

    gathered = lax.all_to_all(
        spread.reshape(T * chips, own, columns), GROUP, split_axis=0, concat_axis=0, tiled=True
    ).reshape(T, chips, own, columns)
    gathered, states = lax.optimization_barrier((gathered, states))
    other_a = swap(gathered[:EARLY], "core")
    other_b = swap(gathered[EARLY:], "core")
    weights, new_master, new_first, new_second = place_own(ids, gathered, states)
    weights = place_other(ids, other_a, 0, weights, "place_early")
    weights = place_other(ids, other_b, EARLY, weights, "place_late")
    return (new_master, new_first, new_second, weights.reshape(rows, columns))


def solution(mesh):
    fine = Mesh(mesh.devices.reshape(Z, X, 2, Y, 2), ("z_hi", "x", "core", "y", "z_lo"))
    owners = DP + TENSOR
    return jax.shard_map(
        local,
        mesh=fine,
        in_specs=(
            P(DP, None, TENSOR),
            P(owners, None),
            P(owners, None),
            P(owners, None),
            P(None, owners, None),
            P(),
            P(),
        ),
        out_specs=(P(owners, None), P(owners, None), P(owners, None), P(None, TENSOR)),
        check_vma=False,
    )
```

```python
import functools

import jax
import jax.numpy as jnp
from jax import lax
from jax.experimental import pallas as pl
from jax.experimental.pallas import tpu as pltpu
from jax.sharding import Mesh, PartitionSpec as P

HISTORY = 16
GROUP = ("y", "z_lo", "z_hi", "x")
DP = ("z_hi", "x", "core")
TENSOR = ("y", "z_lo")
Z, X, Y, T = 2, 4, 4, 8
EARLY = 6
VMEM_BYTES = 16 * 1024 * 1024
SMALL = 1024 * 1024
SMEM = pl.BlockSpec(memory_space=pltpu.SMEM)
ANY = pl.BlockSpec(memory_space=pl.ANY)
VMEM = pl.BlockSpec(memory_space=pltpu.VMEM)
F32, BF16 = jnp.float32, jnp.bfloat16


def struct(shape, dtype):
    return jax.ShapeDtypeStruct(shape, dtype)


def in_hbm(array):
    return pltpu.with_memory_space_constraint(array, pltpu.HBM)


def in_vmem(array):
    return pltpu.with_memory_space_constraint(array, pltpu.VMEM)


def run_copies(copies, sems):
    started = [pltpu.make_async_copy(source, target, sems.at[i]) for i, (source, target) in enumerate(copies)]
    for copy in started:
        copy.start()
    for copy in started:
        copy.wait()


def copying(body, n, out_shape, n_in, aliases=None, moved=0, name=None):
    many = isinstance(out_shape, (tuple, list))

    def kernel(ids_ref, *refs):
        run_copies(body(ids_ref, refs[:n_in], refs[n_in:-1]), refs[-1])

    return pl.pallas_call(
        kernel,
        out_shape=out_shape,
        in_specs=[SMEM] + [ANY] * n_in,
        out_specs=[ANY] * len(out_shape) if many else ANY,
        scratch_shapes=[pltpu.SemaphoreType.DMA((n,))],
        input_output_aliases=aliases or {},
        compiler_params=pltpu.CompilerParams(vmem_limit_bytes=SMALL),
        cost_estimate=pl.CostEstimate(flops=0, bytes_accessed=moved, transcendentals=0),
        name=name,
    )


def split(ids, halves, parts, name):
    rows, columns = halves.shape[2:]

    def body(ids_ref, ins, outs):
        core = ids_ref[2]
        return [
            (ins[0].at[pl.ds(first, n), 1 - core if other else core], outs[i])
            for i, (first, n, other) in enumerate(parts)
        ]

    out = [pltpu.VMEM((n, rows, columns), BF16) for _, n, _ in parts]
    moved = 4 * rows * columns * sum(n for _, n, _ in parts)
    return copying(body, len(parts), out, 1, moved=moved, name=name)(ids, in_hbm(halves))


def place_own(ids, pieces, states):
    owners, chips, rows, columns = pieces.shape

    def body(ids_ref, ins, outs):
        copies = [(ins[0].at[:, i], outs[0].at[i, ids_ref[2]]) for i in range(chips)]
        return copies + list(zip(ins[1:], outs[1:]))

    out = [pltpu.HBM((chips, 2, owners, rows, columns), BF16)] + [pltpu.HBM(a.shape, a.dtype) for a in states]
    moved = 4 * pieces.size + sum(8 * a.size for a in states)
    call = copying(body, chips + len(states), out, 1 + len(states), moved=moved, name="place_own")
    return call(ids, *[in_vmem(a) for a in (pieces, *states)])


def place_other(ids, pieces, first, into, name):
    n = pieces.shape[0]

    def body(ids_ref, ins, outs):
        return [(ins[0].at[t], outs[0].at[:, 1 - ids_ref[2], first + t]) for t in range(n)]

    call = copying(body, n, struct(into.shape, BF16), 2, {2: 0}, 4 * pieces.size, name)
    return call(ids, in_vmem(pieces), into)


def noise_kernel(coeffs_ref, step_ref, draws_ref, noise_ref):
    weights = [
        coeffs_ref[(step_ref[0] - slot) & (HISTORY - 1)].astype(F32) / 32.0 for slot in range(HISTORY)
    ]
    width = 3584

    def part(i, carry):
        cut = pl.ds(pl.multiple_of(i * width, width), width)
        total = None
        for slot in range(HISTORY):
            term = weights[slot] * draws_ref[slot, :, cut].astype(F32)
            total = term if total is None else total + term
        noise_ref[:, cut] = total
        return carry

    lax.fori_loop(0, noise_ref.shape[1] // width, part, 0)


def noise_sum(band_coeffs, step, noise_draws):
    slots, rows, columns = noise_draws.shape
    return pl.pallas_call(
        noise_kernel,
        out_shape=[pltpu.VMEM((rows, columns), F32)],
        in_specs=[SMEM, SMEM, VMEM],
        out_specs=[VMEM],
        compiler_params=pltpu.CompilerParams(vmem_limit_bytes=VMEM_BYTES),
        cost_estimate=pl.CostEstimate(
            flops=2 * slots * rows * columns, bytes_accessed=2 * slots * rows * columns, transcendentals=0
        ),
        name="noise_sum",
    )(band_coeffs, step, in_vmem(noise_draws))[0]


def adam(grad_sum, noise, master, first, second, correct_ref):
    gradient = 0.25 * (grad_sum + noise)
    new_first = 0.9 * first + 0.1 * gradient
    new_second = 0.95 * second + 0.05 * gradient * gradient
    update = new_first / correct_ref[0] / (jnp.sqrt(new_second / correct_ref[1]) + 1e-08) + 0.1 * master
    return master - 0.02 * update, new_first, new_second


def total_of(sums_ref):
    total = sums_ref[0, 0].astype(F32)
    for source in range(1, sums_ref.shape[1]):
        total = total + sums_ref[0, source].astype(F32)
    return total


def adam_kernel(
    correct_ref, sums_ref, noise_ref, master_ref, first_ref, second_ref,
    new_master_ref, new_first_ref, new_second_ref, spread_ref,
):
    new_master, new_first_ref[...], new_second_ref[...] = adam(
        total_of(sums_ref), noise_ref[...], master_ref[...], first_ref[...], second_ref[...], correct_ref
    )
    new_master_ref[...] = new_master
    rounded = new_master.astype(BF16)
    for copy in range(spread_ref.shape[1]):
        spread_ref[0, copy] = rounded


def adam_step(correct, sums, noise, master, first, second):
    parts, sources, rows, width = sums.shape
    state = pl.BlockSpec((rows, width), lambda i: (0, i))
    spread = pl.BlockSpec((1, sources, rows, width), lambda i: (i, 0, 0, 0))
    return pl.pallas_call(
        adam_kernel,
        out_shape=[pltpu.VMEM(master.shape, F32)] * 3 + [pltpu.VMEM(sums.shape, BF16)],
        grid=(parts,),
        in_specs=[SMEM, spread, state, state, state, state],
        out_specs=[state] * 3 + [spread],
        compiler_params=pltpu.CompilerParams(vmem_limit_bytes=VMEM_BYTES),
        name="adam_step",
    )(correct, in_vmem(sums), in_vmem(noise), in_vmem(master), in_vmem(first), in_vmem(second))


def swap(value, axis):
    return lax.ppermute(value, axis, [(0, 1), (1, 0)])


def plus_kernel(n_ids, *refs):
    a_ref, b_ref, out_ref = refs[n_ids], refs[n_ids + 1], refs[-1]
    owners, _, rows, _ = out_ref.shape
    for t in range(owners):
        cut = slice(t * rows, (t + 1) * rows)
        out_ref[t, 0] = (a_ref[0, cut].astype(F32) + b_ref[0, cut].astype(F32)).astype(BF16)


def plus(a, b, first, chips, into=None, ids=None):
    n, rows, columns = a.shape
    block = pl.BlockSpec((1, rows, columns), lambda i: (i, 0, 0))
    more = [] if into is None else [into]
    wait = [] if ids is None else [ids]
    return pl.pallas_call(
        functools.partial(plus_kernel, len(wait)),
        out_shape=[pltpu.VMEM((T, chips, rows // T, columns), BF16)],
        grid=(n,),
        in_specs=[ANY] * len(wait) + [block, block] + [ANY] * len(more),
        out_specs=[pl.BlockSpec((T, 1, rows // T, columns), lambda i: (0, first + i, 0, 0))],
        input_output_aliases={len(wait) + 2: 0} if more else {},
        compiler_params=pltpu.CompilerParams(vmem_limit_bytes=VMEM_BYTES),
        name="plus",
    )(*wait, in_vmem(a), in_vmem(b), *more)[0]


TURN = (("z_hi", "x", "y"), ("x", "y", "z_lo"))
MESH = ("z_hi", "x", "core", "y", "z_lo")
SIZES = {"z_hi": Z, "x": X, "core": 2, "y": Y, "z_lo": 2}


def index_of(place):
    index = 0
    for name in MESH:
        index = index * SIZES[name] + place[name]
    return index


def after_turn(ids, ready):
    token = ids.astype(F32) + 0.0 * ready.reshape(-1)[: ids.shape[0]].astype(F32)
    for axes in TURN:
        pairs = []
        for flat in range(2 * X * Z * T):
            place, rest = {}, flat
            for name in reversed(MESH):
                place[name], rest = rest % SIZES[name], rest // SIZES[name]
            if place["core"] == 1:
                across = dict(place, **{a: (place[a] + SIZES[a] // 2) % SIZES[a] for a in axes})
                pairs.append((flat, index_of(across)))
        token = lax.ppermute(token, MESH, pairs)
    return ids + (token < 0.0).astype(jnp.int32)


def local(partial_grads, master, first, second, noise_draws, band_coeffs, step):
    ids = jnp.stack([lax.axis_index(name) for name in ("z_hi", "x", "core", "y", "z_lo")]).astype(jnp.int32)
    _, rows, columns = partial_grads.shape
    block = rows // (2 * X * Z)
    own = block // T
    halves = partial_grads.reshape(Z * X, 2, block, columns)

    chips = Z * X
    half = chips // 2
    (given_a,) = split(ids, halves, [(0, half, True)], "split_first")
    got_a = swap(given_a, "core")
    given_b, kept_a, kept_b = split(
        ids, halves, [(half, half, True), (0, half, False), (half, half, False)], "split_rest"
    )
    got_b = swap(given_b, "core")

    noise = noise_sum(band_coeffs, step, noise_draws)
    count = (step[0] + 1).astype(F32)
    correct = 1.0 - jnp.power(jnp.array([0.9, 0.95], F32), count)

    pieces = plus(kept_a, got_a, 0, chips)
    pieces = plus(kept_b, got_b, half, chips, pieces, after_turn(ids, got_a[0, 0, :8]))
    pieces, noise, correct = lax.optimization_barrier((pieces, noise, correct))
    sums = lax.all_to_all(
        pieces.reshape(T * chips, own, columns), GROUP, split_axis=0, concat_axis=0, tiled=True
    ).reshape(T, chips, own, columns)
    *states, spread = adam_step(correct, sums, noise, master, first, second)

    gathered = lax.all_to_all(
        spread.reshape(T * chips, own, columns), GROUP, split_axis=0, concat_axis=0, tiled=True
    ).reshape(T, chips, own, columns)
    gathered, states = lax.optimization_barrier((gathered, states))
    other_a = swap(gathered[:EARLY], "core")
    other_b = swap(gathered[EARLY:], "core")
    weights, new_master, new_first, new_second = place_own(ids, gathered, states)
    weights = place_other(ids, other_a, 0, weights, "place_early")
    weights = place_other(ids, other_b, EARLY, weights, "place_late")
    return (new_master, new_first, new_second, weights.reshape(rows, columns))


def solution(mesh):
    fine = Mesh(mesh.devices.reshape(Z, X, 2, Y, 2), ("z_hi", "x", "core", "y", "z_lo"))
    owners = DP + TENSOR
    return jax.shard_map(
        local,
        mesh=fine,
        in_specs=(
            P(DP, None, TENSOR),
            P(owners, None),
            P(owners, None),
            P(owners, None),
            P(None, owners, None),
            P(),
            P(),
        ),
        out_specs=(P(owners, None), P(owners, None), P(owners, None), P(None, TENSOR)),
        check_vma=False,
    )
```
